768 devices in a mesh: row: 96 (over y, z_lo, x), col: 8 (over z_hi, core).
Axes of the slice: x: 4, y: 8, z: 12 (z_hi: 4, z_lo: 3; z = z_hi * 3 + z_lo), core: 2. Of those that a mesh axis runs over, the one named last changes fastest.
Arguments:
- features: bfloat16 [98304, 256], P(('row', 'col')), may hold values from -6 to 6
- weight: float32 [256, 256], replicated, may hold values from -0.375 to 0.375
- bias: float32 [256], replicated, may hold values from -3 to 3
- cotangent: bfloat16 [98304, 256], P(('row', 'col')), may hold values from -6 to 6
- tile_values: bfloat16 [96, 8, 24, 128, 128], P('row', 'col'), may hold values from -0.3125 to 0.3125
- tile_pos: int32 [96, 8, 24], P('row', 'col'), may hold values from 0 to 767, as said below
- tile_count: int32 [96, 8], P('row', 'col'), may hold values from 1 to 24, as said below
Outputs:
- output: bfloat16 [98304, 256], P(('row', 'col'))
- grad_weight: float32 [256, 256], replicated
- grad_bias: float32 [256], replicated
- grad_input: bfloat16 [98304, 256], P(('row', 'col'))
The draws below stay inside these ranges and needn't reach their ends.
Inputs may be any that keep to these rules, and one draw needn't show every extreme that they name: `tile_pos`: the 24 positions of one device are distinct; some device holds positions 0 and 767. `tile_count`: some device uses all 24 slots.
All inputs are finite; a program needn't handle non-finite values.
Results may differ from the reference program's by a relative error of at most 0.008.
Values may be sent and summed in bfloat16 or wider, within the bound.
A program may use at most 64 MiB of HBM per device.

```python
import math
import jax
import jax.numpy as jnp
from jax import lax

FEAT = 256
TILE = 128
NODE_DEV = 128
NODES = 98304
RT = 8
CT = 96
SLOTS = 24
N_ROW = 96
N_COL = 8


def draw_tile_pos(key, part):
    key = jax.random.fold_in(key, 11)
    total = RT * CT
    devices = N_ROW * N_COL
    keys = jax.random.split(key, devices)
    scores = jax.vmap(lambda single: jax.random.permutation(single, total))(keys).astype(jnp.int32)
    chosen = jax.random.randint(jax.random.fold_in(key, 1), (), 0, devices)
    marked = jnp.arange(devices)[:, None] == chosen
    places = jnp.arange(total)[None, :]
    scores = jnp.where(marked & (places == 0), -2, scores)
    scores = jnp.where(marked & (places == total - 1), -1, scores)
    order = jnp.argsort(scores, axis=1, stable=True)[:, :SLOTS]
    return order.reshape(N_ROW, N_COL, SLOTS).astype(jnp.int32)


def draw_tile_count(key, part):
    key = jax.random.fold_in(key, 12)
    counts = jax.random.randint(key, (N_ROW * N_COL,), 1, SLOTS + 1)
    chosen = jax.random.randint(jax.random.fold_in(key, 1), (), 0, N_ROW * N_COL)
    counts = jnp.where(jnp.arange(N_ROW * N_COL) == chosen, SLOTS, counts)
    return counts.reshape(N_ROW, N_COL).astype(jnp.int32)


def levels(own_key, dims, pieces, least, largest):
    def one(dim, parts):
        steps = jax.random.uniform(jax.random.fold_in(jax.random.fold_in(own_key, 6), dim), (parts,), jnp.float32, least / len(pieces), largest / len(pieces))
        return jnp.repeat(jnp.exp(steps), dims[dim] // parts).reshape((-1,) + (1,) * (len(dims) - dim - 1))

    level = one(*pieces[0])
    for cut in pieces[1:]:
        level = level * one(*cut)
    return level


def bell_draw(rng, dims, spread, limit, shards=(), held_as=jnp.bfloat16):
    values = jax.random.normal(rng, dims, jnp.float32) * spread
    if len(shards) > 0:
        values = levels(rng, dims, shards, -0.22, 0.18) * values
    return jnp.clip(values, min=-limit, max=limit).astype(held_as)


def setup_inputs(seed: int = 0) -> dict:
    arg_keys = jax.random.split(jax.random.key(seed), 8)
    features = bell_draw(arg_keys[0], (NODES, FEAT), 1.0, 6.0, ((0, 768),))
    weight = bell_draw(arg_keys[1], (FEAT, FEAT), FEAT ** -0.5, 0.375, (), jnp.float32)
    bias = bell_draw(arg_keys[2], (FEAT,), 0.5, 3.0, (), jnp.float32)
    cotangent = bell_draw(arg_keys[3], (NODES, FEAT), 1.0, 6.0, ((0, 768),))
    tile_values = bell_draw(arg_keys[4], (N_ROW, N_COL, SLOTS, TILE, TILE), (TILE * max(1, SLOTS // RT)) ** -0.5, 0.3125, ((0, 96), (1, 8)))
    tile_pos = draw_tile_pos(jax.random.fold_in(arg_keys[7], 71), 0)
    tile_count = draw_tile_count(jax.random.fold_in(arg_keys[7], 71), 0)
    return {"features": features, "weight": weight, "bias": bias, "cotangent": cotangent, "tile_values": tile_values, "tile_pos": tile_pos, "tile_count": tile_count}


def silu_slope(values):
    sig = jax.nn.sigmoid(values)
    return sig * (1.0 + values * (1.0 - sig))

def reference(features, weight, bias, cotangent, tile_values, tile_pos, tile_count):
    feat_dim = features.shape[1]
    grouped = features.reshape(N_ROW, N_COL, NODE_DEV, feat_dim)
    col_blocks = jnp.transpose(grouped, (1, 0, 2, 3)).reshape(N_COL, CT, TILE, feat_dim)

    def forward_step(device, total):
        row_at = device // N_COL
        col_at = device % N_COL
        tiles_f = tile_values[row_at, col_at].astype(jnp.float32)
        places = tile_pos[row_at, col_at]
        active = (jnp.arange(SLOTS) < tile_count[row_at, col_at]).astype(jnp.float32)
        inputs = col_blocks[col_at][places % CT].astype(jnp.float32)
        product = jnp.einsum('kij,kjf->kif', tiles_f, inputs)
        row_hot = (places[:, None] // CT == jnp.arange(RT)[None, :]).astype(jnp.float32) * active[:, None]
        summed = jnp.einsum('kr,kif->rif', row_hot, product)
        return total.at[row_at].add(summed)
    zeros_row = jnp.zeros((N_ROW, RT, TILE, feat_dim), jnp.float32)
    hidden = lax.fori_loop(0, N_ROW * N_COL, forward_step, zeros_row).reshape(NODES, feat_dim)
    pre_act = jnp.dot(hidden, weight, precision=lax.Precision.HIGHEST) + bias
    output = jax.nn.silu(pre_act).astype(jnp.bfloat16)
    grad_pre = (cotangent.astype(jnp.float32) * silu_slope(pre_act)).astype(jnp.bfloat16)
    factor = 1.0 / math.sqrt(NODES)
    grad_weight = jnp.dot(hidden.T, grad_pre.astype(jnp.float32), precision=lax.Precision.HIGHEST) * factor
    grad_bias = lax.optimization_barrier(jnp.sum(grad_pre.astype(jnp.float32), axis=0)) * factor
    row_blocks = grad_pre.reshape(N_ROW, RT, TILE, feat_dim)

    def backward_step(device, total):
        row_at = device // N_COL
        col_at = device % N_COL
        tiles_f = tile_values[row_at, col_at].astype(jnp.float32)
        places = tile_pos[row_at, col_at]
        active = (jnp.arange(SLOTS) < tile_count[row_at, col_at]).astype(jnp.float32)
        inputs = row_blocks[row_at][places // CT].astype(jnp.float32)
        product = jnp.einsum('kij,kif->kjf', tiles_f, inputs)
        col_hot = (places[:, None] % CT == jnp.arange(CT)[None, :]).astype(jnp.float32) * active[:, None]
        summed = jnp.einsum('kc,kjf->cjf', col_hot, product)
        return total.at[col_at].add(summed)
    zeros_col = jnp.zeros((N_COL, CT, TILE, feat_dim), jnp.float32)
    gathered = lax.fori_loop(0, N_ROW * N_COL, backward_step, zeros_col)
    adjoint = jnp.transpose(gathered.reshape(N_COL, N_ROW, NODE_DEV, feat_dim), (1, 0, 2, 3)).reshape(NODES, feat_dim)
    grad_input = jnp.dot(adjoint, weight.T, precision=lax.Precision.HIGHEST).astype(jnp.bfloat16)
    return (output, grad_weight, grad_bias, grad_input)
```

```python
import math

import jax
import jax.numpy as jnp
from jax import lax
from jax.experimental import pallas as pl
from jax.experimental.pallas import tpu as pltpu
from jax.sharding import PartitionSpec as P

TILE = 128
FEAT = 256
NY, NZ, NX = 8, 3, 4
NH, NC = 4, 2
SLOTS = 24
RT = NH * NC
CT = NY * NZ * NX
CUT = 48
MID = 96
NSEM = 160
MESH = pl.DeviceIdType.MESH
HIGHEST = lax.Precision.HIGHEST
F32 = jnp.float32
BF16 = jnp.bfloat16
FIRST = pl.ds(0, CUT)
SECOND = pl.ds(CUT, TILE - CUT)


def kernel(table, links, feat, weight, bias, cot, vals, out, gw, gb, gin,
           gath, flip, acc, part, hpart, hcore, hline, grow,
           ring_p, line_p, line_q, ring_q, zline,
           wbuf, wcore, wx, wy, wz, wh, wout, ssem, rsem):
    row = lax.axis_index("row")
    col = lax.axis_index("col")
    y, z, x = row // (NZ * NX), (row // NX) % NZ, row % NX
    h, c = col // NC, col % NC

    def at_x(s):
        return lax.rem(x + s + NX, NX)

    def at_y(s):
        return lax.rem(y + s + NY, NY)

    def at_z(s):
        return lax.rem(z + s, NZ)

    def at_h(s):
        return lax.rem(h + s + NH, NH)

    def to_x(s):
        return ((y * NZ + z) * NX + at_x(s), col)

    def to_y(s):
        return ((at_y(s) * NZ + z) * NX + x, col)

    def to_z(s):
        return ((y * NZ + at_z(s)) * NX + x, col)

    def to_h(index):
        return (row, index * NC + c)

    other_core = 1 - c
    partner = (row, h * NC + other_core)
    turn = 1 - 2 * c
    near = at_h(turn)
    back = at_h(-turn)
    far = at_h(2)

    copies = []

    def send(src, dst, target):
        index = len(copies)
        copy = pltpu.make_async_remote_copy(
            src_ref=src, dst_ref=dst, send_sem=ssem.at[index], recv_sem=rsem.at[index],
            device_id=target, device_id_type=MESH)
        copy.start()
        copies.append(copy)
        return copy

    barrier = pltpu.get_barrier_semaphore()
    friends = [to_x(s) for s in (1, 2, 3)] + [to_y(s) for s in range(1, NY)]
    friends += [to_z(s) for s in (1, 2)] + [to_h(at_h(s)) for s in (1, 2, 3)] + [partner]
    for friend in friends:
        pl.semaphore_signal(barrier, inc=1, device_id=friend, device_id_type=MESH)
    gath[y, z, x] = feat[...]
    pl.semaphore_wait(barrier, len(friends))

    zs = [send(feat, gath.at[y, z, x], to_z(s)) for s in (1, 2)]
    acc[SLOTS] = jnp.zeros((TILE, FEAT), F32)
    for k in range(SLOTS):
        flip[k] = vals[k].T
    for cp in zs:
        cp.wait_recv()

    def q_direct(s):
        block = gath.at[at_y(s), :, x, SECOND, :]
        return {1: send(block, block, to_x(1)), -1: send(block, block, to_x(-1))}

    def q_forward(s, arrived):
        way = 1 if s % 2 == 0 else -1
        arrived[way].wait_recv()
        block = gath.at[at_y(s), :, at_x(-way), SECOND, :]
        return [arrived[-way], send(block, block, to_x(way))]

    own_q = gath.at[y, :, x, SECOND, :]
    ring_up = send(own_q, own_q, to_y(1))
    ring_down = send(own_q, own_q, to_y(-1))
    own_p = gath.at[y, :, x, FIRST, :]
    px = [send(own_p, own_p, to_x(s)) for s in (1, 2, 3)]
    direct = {0: q_direct(0)}
    pending = []
    for cp in px:
        cp.wait_recv()
    block = gath.at[y, :, :, FIRST, :]
    p_up = send(block, block, to_y(1))
    p_down = send(block, block, to_y(-1))
    previous = [0]
    for s in (1, 2, 3, 4):
        ring_up.wait_recv()
        ring_down.wait_recv()
        if s < 3:
            block = gath.at[at_y(-s), :, x, SECOND, :]
            ring_up = send(block, block, to_y(1))
            block = gath.at[at_y(s), :, x, SECOND, :]
            ring_down = send(block, block, to_y(-1))
        elif s == 3:
            block = gath.at[at_y(-s), :, x, pl.ds(CUT, MID - CUT), :]
            ring_up = send(block, block, to_y(1))
            block = gath.at[at_y(s), :, x, pl.ds(MID, TILE - MID), :]
            ring_down = send(block, block, to_y(-1))
        current = [-s, s] if s < 4 else [4]
        for t in current:
            direct[t] = q_direct(t)
        for t in previous:
            pending += q_forward(t, direct[t])
        previous = current
        p_up.wait_recv()
        p_down.wait_recv()
        if s < 3:
            block = gath.at[at_y(-s), :, :, FIRST, :]
            p_up = send(block, block, to_y(1))
            block = gath.at[at_y(s), :, :, FIRST, :]
            p_down = send(block, block, to_y(-1))
        elif s == 3:
            block = gath.at[at_y(-s), :, 0:2, FIRST, :]
            p_up = send(block, block, to_y(1))
            block = gath.at[at_y(s), :, 2:4, FIRST, :]
            p_down = send(block, block, to_y(-1))
    for t in previous:
        pending += q_forward(t, direct[t])
    for cp in pending:
        cp.wait_recv()

    for k in range(SLOTS):
        spot = table[1, k]
        block = gath[spot // (NZ * NX), (spot // NX) % NZ, spot % NX]
        value = jnp.dot(vals[k], block, preferred_element_type=F32)
        acc[k] = value + acc[links[k]]
    for r in range(RT):
        hpart[r % NC, r // NC] = acc[links[SLOTS + r]].astype(BF16)

    cp = send(hpart.at[other_core], hcore, partner)
    cp.wait_recv()
    hpart[c] = hpart[c] + hcore[...]
    leg = send(hpart.at[c, far], hline.at[0], to_h(near))
    plain = send(hpart.at[c, back], hline.at[1], to_h(back))
    leg.wait_recv()
    hpart[c, near] = hpart[c, near] + hline[0]
    summed = send(hpart.at[c, near], hline.at[2], to_h(near))
    hidden = acc[links[SLOTS + col]] + hcore[h].astype(F32)
    plain.wait_recv()
    hidden = hidden + hline[1].astype(F32)
    summed.wait_recv()
    hidden = hidden + hline[2].astype(F32)

    pre_act = jnp.dot(hidden, weight[...], precision=HIGHEST, preferred_element_type=F32) + bias[...]
    sig = jax.nn.sigmoid(pre_act)
    slope = sig * (1.0 + pre_act * (1.0 - sig))
    grad_pre = (cot[...].astype(F32) * slope).astype(BF16)
    grow[h, c] = grad_pre

    own = grow.at[h, c]
    ahead = send(own, own, to_h(near))
    behind = send(own, own, to_h(back))
    over = [send(own, own, partner)]
    out[...] = (pre_act * sig).astype(BF16)
    factor = 1.0 / math.sqrt(TILE * NY * NZ * NX * NH * NC)
    grad_float = grad_pre.astype(F32)
    local = lax.dot_general(hidden, grad_float, (((0,), (0,)), ((), ())), precision=HIGHEST,
                            preferred_element_type=F32)
    local_bias = jnp.sum(grad_float, axis=0, keepdims=True)
    for cc in range(NC):
        cols = slice(cc * TILE, (cc + 1) * TILE)
        wbuf[cc, :, :, 0:8, :] = local[:, cols].reshape(NX, NY, 8, TILE)
        wbuf[cc, :, :, 8:16, :] = jnp.broadcast_to(local_bias[:, cols].reshape(1, 1, 1, TILE), (NX, NY, 8, TILE))
    ahead.wait_recv()
    block = grow.at[back, c]
    onward = send(block, block, to_h(near))
    over.append(send(block, block, partner))
    behind.wait_recv()
    block = grow.at[near, c]
    over.append(send(block, block, partner))
    w_core = send(wbuf.at[other_core], wcore, partner)
    onward.wait_recv()
    block = grow.at[far, c]
    over.append(send(block, block, partner))
    for cp in over:
        cp.wait_recv()

    for k in range(SLOTS):
        spot = table[0, k]
        value = jnp.dot(flip[k], grow[spot // NC, spot % NC], preferred_element_type=F32)
        acc[k] = value + acc[links[SLOTS + RT + k]]

    def fill(s):
        yd = at_y(s)
        for zi in range(NZ):
            for xi in range(NX):
                place = (yd * NZ + zi) * NX + xi
                part[yd, zi, xi] = acc[links[2 * SLOTS + RT + place]].astype(BF16)

    def add(dst, src):
        dst[...] = dst[...] + src[...]

    def q_start(s):
        way = 1 if s % 2 == 0 else -1
        place = len(lines)
        lines[s] = way, place
        leg = send(part.at[at_y(s), :, at_x(2), SECOND, :], line_q.at[place, 0], to_x(way))
        straight = send(part.at[at_y(s), :, at_x(-way), SECOND, :], line_q.at[place, 1], to_x(-way))
        return leg, straight

    def q_middle(s, leg):
        way, place = lines[s]
        leg.wait_recv()
        block = part.at[at_y(s), :, at_x(way), SECOND, :]
        add(block, line_q.at[place, 0])
        return send(block, line_q.at[place, 2], to_x(way))

    def q_end(s, straight, summed):
        way, place = lines[s]
        straight.wait_recv()
        summed.wait_recv()
        block = part.at[at_y(s), :, x, SECOND, :]
        block[...] = block[...] + line_q[place, 1] + line_q[place, 2]

    lines = {}
    fill(4)
    ring_up = send(part.at[at_y(4), :, 0:2, FIRST, :], ring_p.at[0, 0, :, 0:2], to_y(1))
    ring_down = send(part.at[at_y(4), :, 2:4, FIRST, :], ring_p.at[1, 0, :, 2:4], to_y(-1))
    started = {4: q_start(4)}
    for s in (3, -3, 2, -2, 1, -1, 0):
        fill(s)
        started[s] = q_start(s)
    middle = {4: q_middle(4, started[4][0])}

    w_core.wait_recv()
    add(wbuf.at[c], wcore)
    w_x = [send(wbuf.at[c, at_x(s)], wx.at[s - 1], to_x(s)) for s in (1, 2, 3)]

    q_up = q_down = None
    for t in (0, 1, 2, 3, 4):
        group = [4] if t == 0 else ([4 - t, t - 4] if t < 4 else [0])
        after = [] if t == 4 else ([3 - t, t - 3] if t < 3 else [0])
        for s in after:
            middle[s] = q_middle(s, started[s][0])
        if t >= 1:
            ring_up.wait_recv()
            ring_down.wait_recv()
            if t == 1:
                add(part.at[at_y(3), :, 0:2, FIRST, :], ring_p.at[0, 0, :, 0:2])
                add(part.at[at_y(-3), :, 2:4, FIRST, :], ring_p.at[1, 0, :, 2:4])
            else:
                add(part.at[at_y(4 - t), :, :, FIRST, :], ring_p.at[0, t - 1])
                add(part.at[at_y(t - 4), :, :, FIRST, :], ring_p.at[1, t - 1])
            if t < 4:
                ring_up = send(part.at[at_y(4 - t), :, :, FIRST, :], ring_p.at[0, t], to_y(1))
                ring_down = send(part.at[at_y(t - 4), :, :, FIRST, :], ring_p.at[1, t], to_y(-1))
            else:
                px = [send(part.at[y, :, at_x(s), FIRST, :], line_p.at[s - 1], to_x(s)) for s in (1, 2, 3)]
        for s in group:
            q_end(s, started[s][1], middle[s])
        if t == 0:
            q_up = send(part.at[at_y(4), :, x, pl.ds(CUT, MID - CUT), :],
                        ring_q.at[0, 0, :, pl.ds(0, MID - CUT), :], to_y(1))
            q_down = send(part.at[at_y(4), :, x, pl.ds(MID, TILE - MID), :],
                          ring_q.at[1, 0, :, pl.ds(MID - CUT, TILE - MID), :], to_y(-1))
        else:
            q_up.wait_recv()
            q_down.wait_recv()
            if t == 1:
                add(part.at[at_y(3), :, x, pl.ds(CUT, MID - CUT), :], ring_q.at[0, 0, :, pl.ds(0, MID - CUT), :])
                add(part.at[at_y(-3), :, x, pl.ds(MID, TILE - MID), :],
                    ring_q.at[1, 0, :, pl.ds(MID - CUT, TILE - MID), :])
            else:
                add(part.at[at_y(4 - t), :, x, SECOND, :], ring_q.at[0, t - 1])
                add(part.at[at_y(t - 4), :, x, SECOND, :], ring_q.at[1, t - 1])
            if t < 4:
                q_up = send(part.at[at_y(4 - t), :, x, SECOND, :], ring_q.at[0, t], to_y(1))
                q_down = send(part.at[at_y(t - 4), :, x, SECOND, :], ring_q.at[1, t], to_y(-1))
        if t == 0:
            for cp in w_x:
                cp.wait_recv()
            wbuf[c, x] = wbuf[c, x] + wx[0] + wx[1] + wx[2]
            w_y = [send(wbuf.at[c, x, at_y(s)], wy.at[s - 1], to_y(s)) for s in range(1, NY)]
        elif t == 1:
            for cp in w_y:
                cp.wait_recv()
            wz[z] = wbuf[c, x, y] + jnp.sum(wy[...], axis=0)
            w_z = [send(wz.at[z], wz.at[z], to_z(s)) for s in (1, 2)]
        elif t == 2:
            for cp in w_z:
                cp.wait_recv()
            wh[h] = wz[0] + wz[1] + wz[2]
            w_h = [send(wh.at[h], wh.at[h], to_h(at_h(s))) for s in (1, 2, 3)]
        elif t == 3:
            for cp in w_h:
                cp.wait_recv()
            wout[c, x, y] = (wh[0] + wh[1] + wh[2] + wh[3]) * factor
            piece = wout.at[c, x, y]
            w_y = [send(piece, piece, to_y(s)) for s in range(1, NY)]
        else:
            for cp in w_y:
                cp.wait_recv()
            piece = wout.at[c, x]
            w_x = [send(piece, piece, to_x(s)) for s in (1, 2, 3)]
    for cp in px:
        cp.wait_recv()
    block = part.at[y, :, x, FIRST, :]
    block[...] = block[...] + line_p[0] + line_p[1] + line_p[2]
    last = [send(part.at[y, at_z(s), x], zline.at[s - 1], to_z(s)) for s in (1, 2)]
    for cp in w_x:
        cp.wait_recv()
    w_core = send(wout.at[c], wout.at[c], partner)
    for cp in last:
        cp.wait_recv()
    adjoint = part[y, z, x].astype(F32) + zline[0].astype(F32) + zline[1].astype(F32)
    gin[...] = lax.dot_general(adjoint, weight[...], (((1,), (1,)), ((), ())), precision=HIGHEST,
                               preferred_element_type=F32).astype(BF16)
    w_core.wait_recv()
    for cc in range(NC):
        cols = slice(cc * TILE, (cc + 1) * TILE)
        gw[:, cols] = wout[cc, :, :, 0:8, :].reshape(FEAT, TILE)
        gb[:, cols] = wout[cc, 0, 0, 8:9, :]
    for cp in copies:
        cp.wait_send()


def per_device(features, weight, bias, cotangent, tile_values, tile_pos, tile_count):
    places = tile_pos[0, 0]
    in_use = tile_count[0, 0]
    slot = jnp.arange(SLOTS, dtype=jnp.int32)
    rows, cols = places // CT, places % CT
    full = jnp.full((CT,), SLOTS, jnp.int32)
    asked = jnp.concatenate([rows, jnp.arange(RT, dtype=jnp.int32), cols + RT, jnp.arange(CT, dtype=jnp.int32) + RT])
    limit = jnp.concatenate([slot, full[:RT], slot, full])
    limit = jnp.minimum(limit, in_use)
    same = jnp.where(asked[:, None] < RT, rows[None, :] == asked[:, None], cols[None, :] + RT == asked[:, None])
    found = jnp.max(jnp.where(same & (slot[None, :] < limit[:, None]), slot[None, :], -1), axis=1)
    links = jnp.where(found < 0, SLOTS, found)
    table = jnp.stack([rows, cols])
    vmem = pl.BlockSpec(memory_space=pltpu.VMEM)
    smem = pl.BlockSpec(memory_space=pltpu.SMEM)
    blocks = pltpu.VMEM
    scratch = [
        blocks((NY, NZ, NX, TILE, FEAT), BF16),
        blocks((SLOTS, TILE, TILE), BF16),
        blocks((SLOTS + 1, TILE, FEAT), F32),
        blocks((NY, NZ, NX, TILE, FEAT), BF16),
        blocks((NC, NH, TILE, FEAT), BF16),
        blocks((NH, TILE, FEAT), BF16),
        blocks((3, TILE, FEAT), BF16),
        blocks((NH, NC, TILE, FEAT), BF16),
        blocks((2, 4, NZ, NX, CUT, FEAT), BF16),
        blocks((3, NZ, CUT, FEAT), BF16),
        blocks((NY, 3, NZ, TILE - CUT, FEAT), BF16),
        blocks((2, 4, NZ, TILE - CUT, FEAT), BF16),
        blocks((2, TILE, FEAT), BF16),
        blocks((NC, NX, NY, 16, TILE), F32),
        blocks((NX, NY, 16, TILE), F32),
        blocks((3, NY, 16, TILE), F32),
        blocks((NY - 1, 16, TILE), F32),
        blocks((NZ, 16, TILE), F32),
        blocks((NH, 16, TILE), F32),
        blocks((NC, NX, NY, 16, TILE), F32),
        pltpu.SemaphoreType.DMA((NSEM,)),
        pltpu.SemaphoreType.DMA((NSEM,)),
    ]
    output, grad_weight, grad_bias, grad_input = pl.pallas_call(
        kernel,
        out_shape=(
            jax.ShapeDtypeStruct((TILE, FEAT), BF16),
            jax.ShapeDtypeStruct((FEAT, FEAT), F32),
            jax.ShapeDtypeStruct((1, FEAT), F32),
            jax.ShapeDtypeStruct((TILE, FEAT), BF16),
        ),
        in_specs=[smem, smem] + [vmem] * 5,
        out_specs=(vmem,) * 4,
        scratch_shapes=scratch,
        compiler_params=pltpu.CompilerParams(
            collective_id=0, has_side_effects=True, vmem_limit_bytes=48 * 1024 * 1024),
    )(table, links, features, weight, bias.reshape(1, FEAT), cotangent, tile_values[0, 0])
    return output, grad_weight, grad_bias[0], grad_input


def solution(mesh):
    in_specs = (
        P(("row", "col"), None),
        P(),
        P(),
        P(("row", "col"), None),
        P("row", "col", None, None, None),
        P("row", "col", None),
        P("row", "col"),
    )
    out_specs = (P(("row", "col"), None), P(), P(), P(("row", "col"), None))
    return jax.shard_map(
        per_device, mesh=mesh, in_specs=in_specs, out_specs=out_specs, check_vma=False
    )
```

```python
import math

import jax
import jax.numpy as jnp
from jax import lax
from jax.experimental import pallas as pl
from jax.experimental.pallas import tpu as pltpu
from jax.sharding import PartitionSpec as P

TILE = 128
FEAT = 256
NY, NZ, NX = 8, 3, 4
NH, NC = 4, 2
SLOTS = 24
RT = NH * NC
CT = NY * NZ * NX
NSEM = 240
MESH = pl.DeviceIdType.MESH
HIGHEST = lax.Precision.HIGHEST
F32 = jnp.float32
BF16 = jnp.bfloat16
FIRST = pl.ds(0, 32)
SECOND = pl.ds(32, 64)
UPPER = pl.ds(32, 32)
LOWER = pl.ds(64, 32)
THIRD = pl.ds(96, 32)
AHEAD = pl.ds(0, 96)
GROUPS = ((4,), (3, -3), (2, -2), (1, -1), (0,))


def way_of(s):
    return 1 if s > 0 else -1


def kernel(places, links, feat_in, weight_in, bias_in, cot_in, vals_in, out_to, gw_to, gb_to, gin_to,
           out, gw, gb, gin, weight, bias, cot, vals,
           gath, flip, acc, part, hpart, hcore, hline, grow,
           ring_p, line_p, line_q, ring_q, line_c, ring_c, last_c, zline,
           wbuf, wcore, wx, wy, wz, wh, wout, ssem, rsem, lsem):
    row = lax.axis_index("row")
    col = lax.axis_index("col")
    y, z, x = row // (NZ * NX), (row // NX) % NZ, row % NX
    h, c = col // NC, col % NC

    def at_x(s):
        return lax.rem(x + s + NX, NX)

    def at_y(s):
        return lax.rem(y + s + NY, NY)

    def at_z(s):
        return lax.rem(z + s, NZ)

    def at_h(s):
        return lax.rem(h + s + NH, NH)

    def to_x(s):
        return ((y * NZ + z) * NX + at_x(s), col)

    def to_y(s):
        return ((at_y(s) * NZ + z) * NX + x, col)

    def to_z(s):
        return ((y * NZ + at_z(s)) * NX + x, col)

    def to_h(index):
        return (row, index * NC + c)

    other_core = 1 - c
    partner = (row, h * NC + other_core)
    turn = 1 - 2 * c
    near = at_h(turn)
    back = at_h(-turn)
    far = at_h(2)

    copies = []

    def send(src, dst, target):
        index = len(copies)
        copy = pltpu.make_async_remote_copy(
            src_ref=src, dst_ref=dst, send_sem=ssem.at[index], recv_sem=rsem.at[index],
            device_id=target, device_id_type=MESH)
        copy.start()
        copies.append(copy)
        return copy

    def fetch(src, dst, index):
        copy = pltpu.make_async_copy(src, dst, lsem.at[index])
        copy.start()
        return copy

    barrier = pltpu.get_barrier_semaphore()
    friends = [to_x(s) for s in (1, 2, 3)] + [to_y(s) for s in range(1, NY)]
    friends += [to_z(s) for s in (1, 2)] + [to_h(at_h(s)) for s in (1, 2, 3)] + [partner]
    for friend in friends:
        pl.semaphore_signal(barrier, inc=1, device_id=friend, device_id_type=MESH)
    own_copy = fetch(feat_in, gath.at[y, z, x], 0)
    fetched = [fetch(vals_in, vals, 1), fetch(weight_in, weight, 2), fetch(cot_in, cot, 3), fetch(bias_in, bias, 4)]
    acc[SLOTS] = jnp.zeros((TILE, FEAT), F32)
    own_copy.wait()
    pl.semaphore_wait(barrier, len(friends))

    def both(up, down):
        return send(up, up, to_y(1)), send(down, down, to_y(-1))

    def ring(view, half, s, arrived):
        for cp in arrived:
            cp.wait_recv()
        if s < 3:
            return both(view(at_y(-s)), view(at_y(s)))
        if s == 3:
            return both(half(at_y(-s), 0), half(at_y(s), 1))
        return None

    def p_view(yd):
        return gath.at[yd, :, :, FIRST, :]

    def p_half(yd, i):
        return gath.at[yd, :, 2 * i:2 * i + 2, FIRST, :]

    def q_view(yd):
        return gath.at[yd, :, x, SECOND, :]

    def q_half(yd, i):
        return gath.at[yd, :, x, (UPPER, LOWER)[i], :]

    def c_view(yd):
        return gath.at[yd, z, :, THIRD, :]

    def c_half(yd, i):
        return gath.at[yd, z, 2 * i:2 * i + 2, THIRD, :]

    def q_direct(s):
        block = gath.at[at_y(s), :, x, SECOND, :]
        return {1: send(block, block, to_x(1)), -1: send(block, block, to_x(-1))}

    def q_forward(s, arrived):
        way = way_of(s)
        arrived[way].wait_recv()
        block = gath.at[at_y(s), :, at_x(-way), SECOND, :]
        return [arrived[-way], send(block, block, to_x(way))]

    def c_direct(s):
        block = gath.at[at_y(s), z, :, THIRD, :]
        return [send(block, block, to_z(1)), send(block, block, to_z(2))]

    own = gath.at[y, z, x, AHEAD, :]
    zs = [send(own, own, to_z(s)) for s in (1, 2)]
    own = gath.at[y, z, x, THIRD, :]
    xs = [send(own, own, to_x(s)) for s in (1, 2, 3)]
    pending = []
    for cp in zs:
        cp.wait_recv()
    q_ring = both(q_view(y), q_view(y))
    own = gath.at[y, :, x, FIRST, :]
    px = [send(own, own, to_x(s)) for s in (1, 2, 3)]
    for cp in xs:
        cp.wait_recv()
    c_ring = both(c_view(y), c_view(y))
    direct = {0: q_direct(0)}
    pending += c_direct(0)
    fetched[0].wait()
    p_ring = None
    for s in (1, 2, 3, 4):
        current = GROUPS[4 - s]
        q_ring = ring(q_view, q_half, s, q_ring)
        for t in current:
            direct[t] = q_direct(t)
        c_ring = ring(c_view, c_half, s, c_ring)
        for t in current:
            pending += c_direct(t)
        if s == 1:
            for cp in px:
                cp.wait_recv()
            p_ring = both(p_view(y), p_view(y))
        for t in GROUPS[5 - s]:
            pending += q_forward(t, direct[t])
        if s > 1:
            p_ring = ring(p_view, p_half, s - 1, p_ring)
        for k in range(6 * s - 6, 6 * s):
            flip[k] = vals[k].T
    pending += q_forward(4, direct[4])
    ring(p_view, p_half, 4, p_ring)
    for cp in pending:
        cp.wait_recv()

    for k in range(SLOTS):
        spot = places[k] % CT
        block = gath[spot // (NZ * NX), (spot // NX) % NZ, spot % NX]
        value = jnp.dot(vals[k], block, preferred_element_type=F32)
        acc[k] = value + acc[links[k]]
    for r in range(RT):
        hpart[r % NC, r // NC] = acc[links[SLOTS + r]].astype(BF16)

    cp = send(hpart.at[other_core], hcore, partner)
    cp.wait_recv()
    hpart[c] = hpart[c] + hcore[...]
    leg = send(hpart.at[c, far], hline.at[0], to_h(near))
    plain = send(hpart.at[c, back], hline.at[1], to_h(back))
    leg.wait_recv()
    hpart[c, near] = hpart[c, near] + hline[0]
    summed = send(hpart.at[c, near], hline.at[2], to_h(near))
    hidden = acc[links[SLOTS + col]] + hcore[h].astype(F32)
    plain.wait_recv()
    hidden = hidden + hline[1].astype(F32)
    summed.wait_recv()
    hidden = hidden + hline[2].astype(F32)

    for cp in fetched[1:]:
        cp.wait()
    pre_act = jnp.dot(hidden, weight[...], precision=HIGHEST, preferred_element_type=F32) + bias[...]
    sig = jax.nn.sigmoid(pre_act)
    slope = sig * (1.0 + pre_act * (1.0 - sig))
    grad_pre = (cot[...].astype(F32) * slope).astype(BF16)
    grow[h, c] = grad_pre

    own = grow.at[h, c]
    ahead = send(own, own, to_h(near))
    behind = send(own, own, to_h(back))
    over = [send(own, own, partner)]
    out[...] = (pre_act * sig).astype(BF16)
    stored = [fetch(out, out_to, 5)]
    factor = 1.0 / math.sqrt(TILE * NY * NZ * NX * NH * NC)
    grad_float = grad_pre.astype(F32)
    local = lax.dot_general(hidden, grad_float, (((0,), (0,)), ((), ())), precision=HIGHEST,
                            preferred_element_type=F32)
    local_bias = jnp.sum(grad_float, axis=0, keepdims=True)
    for cc in range(NC):
        cols = slice(cc * TILE, (cc + 1) * TILE)
        wbuf[cc, :, :, 0:8, :] = local[:, cols].reshape(NX, NY, 8, TILE)
        wbuf[cc, :, :, 8:16, :] = jnp.broadcast_to(local_bias[:, cols].reshape(1, 1, 1, TILE), (NX, NY, 8, TILE))
    w_core = send(wbuf.at[other_core], wcore, partner)
    ahead.wait_recv()
    block = grow.at[back, c]
    onward = send(block, block, to_h(near))
    over.append(send(block, block, partner))
    behind.wait_recv()
    block = grow.at[near, c]
    over.append(send(block, block, partner))
    w_core.wait_recv()
    wbuf[c] = wbuf[c] + wcore[...]
    w_x = [send(wbuf.at[c, at_x(s)], wx.at[s - 1], to_x(s)) for s in (1, 2, 3)]
    onward.wait_recv()
    block = grow.at[far, c]
    over.append(send(block, block, partner))
    for cp in w_x:
        cp.wait_recv()
    wbuf[c, x] = wbuf[c, x] + wx[0] + wx[1] + wx[2]
    w_y = [send(wbuf.at[c, x, at_y(s)], wy.at[s - 1], to_y(s)) for s in range(1, NY)]
    for cp in over:
        cp.wait_recv()

    for k in range(SLOTS):
        spot = places[k] // CT
        value = jnp.dot(flip[k], grow[spot // NC, spot % NC], preferred_element_type=F32)
        acc[k] = value + acc[links[SLOTS + RT + k]]

    def fill(s):
        yd = at_y(s)
        for zi in range(NZ):
            for xi in range(NX):
                place = (yd * NZ + zi) * NX + xi
                part[yd, zi, xi] = acc[links[2 * SLOTS + RT + place]].astype(BF16)

    def add(dst, src):
        dst[...] = dst[...] + src[...]

    def add3(dst, one, two):
        dst[...] = (dst[...].astype(F32) + one[...].astype(F32) + two[...].astype(F32)).astype(BF16)

    def q_start(s):
        way, place = way_of(s), len(started)
        leg = send(part.at[at_y(s), :, at_x(2), SECOND, :], line_q.at[place, 0], to_x(way))
        straight = send(part.at[at_y(s), :, at_x(-way), SECOND, :], line_q.at[place, 1], to_x(-way))
        lines = [send(part.at[at_y(s), at_z(d), :, THIRD, :], line_c.at[place, d - 1], to_z(d)) for d in (1, 2)]
        started[s] = place, leg, straight, lines

    def q_middle(s):
        way = way_of(s)
        place, leg, _, _ = started[s]
        leg.wait_recv()
        block = part.at[at_y(s), :, at_x(way), SECOND, :]
        add(block, line_q.at[place, 0])
        middle[s] = send(block, line_q.at[place, 2], to_x(way))

    def q_end(s):
        place, _, straight, _ = started[s]
        straight.wait_recv()
        middle[s].wait_recv()
        add3(part.at[at_y(s), :, x, SECOND, :], line_q.at[place, 1], line_q.at[place, 2])

    def c_end(s):
        place, _, _, lines = started[s]
        for cp in lines:
            cp.wait_recv()
        add3(part.at[at_y(s), z, :, THIRD, :], line_c.at[place, 0], line_c.at[place, 1])

    def ring_sum(view, half, slot, slot_half, t, arrived):
        if t >= 1:
            for cp in arrived:
                cp.wait_recv()
            if t == 1:
                add(half(at_y(3), 0), slot_half(0))
                add(half(at_y(-3), 1), slot_half(1))
            elif t < 4:
                add(view(at_y(4 - t)), slot(0, t - 1))
                add(view(at_y(t - 4)), slot(1, t - 1))
            else:
                add3(view(y), slot(0, 3), slot(1, 3))
        if t == 0:
            return send(half(at_y(4), 0), slot_half(0), to_y(1)), send(half(at_y(4), 1), slot_half(1), to_y(-1))
        if t < 4:
            return (send(view(at_y(4 - t)), slot(0, t), to_y(1)), send(view(at_y(t - 4)), slot(1, t), to_y(-1)))
        return None

    p_args = (lambda yd: part.at[yd, :, :, FIRST, :],
              lambda yd, i: part.at[yd, :, 2 * i:2 * i + 2, FIRST, :],
              lambda i, t: ring_p.at[i, t],
              lambda i: ring_p.at[i, 0, :, 2 * i:2 * i + 2])
    q_args = (lambda yd: part.at[yd, :, x, SECOND, :],
              lambda yd, i: part.at[yd, :, x, (UPPER, LOWER)[i], :],
              lambda i, t: ring_q.at[i, t],
              lambda i: ring_q.at[i, 0, :, pl.ds(32 * i, 32)])
    c_args = (lambda yd: part.at[yd, z, :, THIRD, :],
              lambda yd, i: part.at[yd, z, 2 * i:2 * i + 2, THIRD, :],
              lambda i, t: ring_c.at[i, t],
              lambda i: ring_c.at[i, 0, 2 * i:2 * i + 2])
    started, middle = {}, {}
    fill(4)
    p_ring = ring_sum(*p_args, 0, None)
    q_start(4)
    for group in GROUPS[1:]:
        for s in group:
            fill(s)
        if group[0] == 3:
            for s in group:
                q_start(s)
    q_middle(4)

    for cp in w_y:
        cp.wait_recv()
    wz[z] = wbuf[c, x, y] + jnp.sum(wy[...], axis=0)
    w_z = [send(wz.at[z], wz.at[z], to_z(s)) for s in (1, 2)]

    q_ring = c_ring = None
    for t in (0, 1, 2, 3, 4):
        if t < 3:
            for s in GROUPS[t + 2]:
                q_start(s)
        if t >= 1:
            p_ring = ring_sum(*p_args, t, p_ring)
        if t == 4:
            px = [send(part.at[y, :, at_x(s), FIRST, :], line_p.at[s - 1], to_x(s)) for s in (1, 2, 3)]
        for s in GROUPS[t]:
            c_end(s)
        c_ring = ring_sum(*c_args, t, c_ring)
        for s in GROUPS[t]:
            q_end(s)
        q_ring = ring_sum(*q_args, t, q_ring)
        if t < 4:
            for s in GROUPS[t + 1]:
                q_middle(s)
        if t == 0:
            for cp in w_z:
                cp.wait_recv()
            wh[h] = wz[0] + wz[1] + wz[2]
            w_h = [send(wh.at[h], wh.at[h], to_h(at_h(s))) for s in (1, 2, 3)]
        elif t == 1:
            for cp in w_h:
                cp.wait_recv()
            wout[c, x, y] = (wh[0] + wh[1] + wh[2] + wh[3]) * factor
            piece = wout.at[c, x, y]
            w_y = [send(piece, piece, to_y(s)) for s in range(1, NY)]
        elif t == 2:
            for cp in w_y:
                cp.wait_recv()
            piece = wout.at[c, x]
            w_x = [send(piece, piece, to_x(s)) for s in (1, 2, 3)]
        elif t == 3:
            for cp in w_x:
                cp.wait_recv()
            w_core = send(wout.at[c], wout.at[c], partner)
    last_q = [send(part.at[y, at_z(s), x, SECOND, :], zline.at[s - 1, SECOND, :], to_z(s)) for s in (1, 2)]
    last_x = [send(part.at[y, z, at_x(s), THIRD, :], last_c.at[s - 1], to_x(s)) for s in (1, 2, 3)]
    for cp in px:
        cp.wait_recv()
    block = part.at[y, :, x, FIRST, :]
    block[...] = (block[...].astype(F32) + line_p[0].astype(F32) + line_p[1].astype(F32)
                  + line_p[2].astype(F32)).astype(BF16)
    last_p = [send(part.at[y, at_z(s), x, FIRST, :], zline.at[s - 1, FIRST, :], to_z(s)) for s in (1, 2)]
    w_core.wait_recv()
    for cc in range(NC):
        cols = slice(cc * TILE, (cc + 1) * TILE)
        gw[:, cols] = wout[cc, :, :, 0:8, :].reshape(FEAT, TILE)
        gb[:, cols] = wout[cc, 0, 0, 8:9, :]
    stored += [fetch(gw, gw_to, 7), fetch(gb, gb_to, 8)]
    for cp in last_q + last_x + last_p:
        cp.wait_recv()
    ahead_rows = part[y, z, x, AHEAD, :].astype(F32) + zline[0].astype(F32) + zline[1].astype(F32)
    third_rows = part[y, z, x, THIRD, :].astype(F32) + last_c[0].astype(F32) + last_c[1].astype(F32)
    third_rows = third_rows + last_c[2].astype(F32)
    adjoint = jnp.concatenate([ahead_rows, third_rows], axis=0)
    gin[...] = lax.dot_general(adjoint, weight[...], (((1,), (1,)), ((), ())), precision=HIGHEST,
                               preferred_element_type=F32).astype(BF16)
    stored.append(fetch(gin, gin_to, 6))
    for cp in copies:
        cp.wait_send()
    for cp in stored:
        cp.wait()


def hand_over(*refs):
    given, wanted, kept, sems = refs[0:4], refs[4:8], refs[8:12], refs[12]
    moves = [pltpu.make_async_copy(given[i], kept[i], sems.at[i]) for i in range(4)]
    for move in moves:
        move.start()
    for i in range(4):
        moves[i].wait()
        moves.append(pltpu.make_async_copy(kept[i], wanted[i], sems.at[4 + i]))
        moves[4 + i].start()
    for move in moves[4:]:
        move.wait()


def per_device(features, weight, bias, cotangent, tile_values, tile_pos, tile_count):
    places = tile_pos[0, 0]
    in_use = tile_count[0, 0]
    slot = jnp.arange(SLOTS, dtype=jnp.int32)
    rows, cols = places // CT, places % CT
    full = jnp.full((CT,), SLOTS, jnp.int32)
    asked = jnp.concatenate([rows, jnp.arange(RT, dtype=jnp.int32), cols + RT, jnp.arange(CT, dtype=jnp.int32) + RT])
    limit = jnp.concatenate([slot, full[:RT], slot, full])
    limit = jnp.minimum(limit, in_use)
    same = jnp.where(asked[:, None] < RT, rows[None, :] == asked[:, None], cols[None, :] + RT == asked[:, None])
    found = jnp.max(jnp.where(same & (slot[None, :] < limit[:, None]), slot[None, :], -1), axis=1)
    links = jnp.where(found < 0, SLOTS, found)
    smem = pl.BlockSpec(memory_space=pltpu.SMEM)
    blocks = pltpu.VMEM
    scratch = [
        blocks((TILE, FEAT), BF16),
        blocks((FEAT, FEAT), F32),
        blocks((1, FEAT), F32),
        blocks((TILE, FEAT), BF16),
        blocks((FEAT, FEAT), F32),
        blocks((1, FEAT), F32),
        blocks((TILE, FEAT), BF16),
        blocks((SLOTS, TILE, TILE), BF16),
        blocks((NY, NZ, NX, TILE, FEAT), BF16),
        blocks((SLOTS, TILE, TILE), BF16),
        blocks((SLOTS + 1, TILE, FEAT), F32),
        blocks((NY, NZ, NX, TILE, FEAT), BF16),
        blocks((NC, NH, TILE, FEAT), BF16),
        blocks((NH, TILE, FEAT), BF16),
        blocks((3, TILE, FEAT), BF16),
        blocks((NH, NC, TILE, FEAT), BF16),
        blocks((2, 4, NZ, NX, 32, FEAT), BF16),
        blocks((3, NZ, 32, FEAT), BF16),
        blocks((NY, 3, NZ, 64, FEAT), BF16),
        blocks((2, 4, NZ, 64, FEAT), BF16),
        blocks((NY, 2, NX, 32, FEAT), BF16),
        blocks((2, 4, NX, 32, FEAT), BF16),
        blocks((3, 32, FEAT), BF16),
        blocks((2, 96, FEAT), BF16),
        blocks((NC, NX, NY, 16, TILE), F32),
        blocks((NX, NY, 16, TILE), F32),
        blocks((3, NY, 16, TILE), F32),
        blocks((NY - 1, 16, TILE), F32),
        blocks((NZ, 16, TILE), F32),
        blocks((NH, 16, TILE), F32),
        blocks((NC, NX, NY, 16, TILE), F32),
        pltpu.SemaphoreType.DMA((NSEM,)),
        pltpu.SemaphoreType.DMA((NSEM,)),
        pltpu.SemaphoreType.DMA((9,)),
    ]
    results = (
        jax.ShapeDtypeStruct((TILE, FEAT), BF16),
        jax.ShapeDtypeStruct((FEAT, FEAT), F32),
        jax.ShapeDtypeStruct((1, FEAT), F32),
        jax.ShapeDtypeStruct((TILE, FEAT), BF16),
    )
    anywhere = pl.BlockSpec(memory_space=pl.ANY)
    made = pl.pallas_call(
        kernel,
        out_shape=results,
        in_specs=[smem, smem] + [anywhere] * 5,
        out_specs=(anywhere,) * 4,
        scratch_shapes=scratch,
        compiler_params=pltpu.CompilerParams(
            collective_id=0, has_side_effects=True, vmem_limit_bytes=63 * 1024 * 1024),
    )(places, links, features, weight, bias.reshape(1, FEAT), cotangent, tile_values[0, 0])
    output, grad_weight, grad_bias, grad_input = pl.pallas_call(
        hand_over,
        out_shape=results,
        in_specs=[anywhere] * 4,
        out_specs=(anywhere,) * 4,
        scratch_shapes=scratch[:4] + [pltpu.SemaphoreType.DMA((8,))],
    )(*made)
    return output, grad_weight, grad_bias[0], grad_input


def solution(mesh):
    in_specs = (
        P(("row", "col"), None),
        P(),
        P(),
        P(("row", "col"), None),
        P("row", "col", None, None, None),
        P("row", "col", None),
        P("row", "col"),
    )
    out_specs = (P(("row", "col"), None), P(), P(), P(("row", "col"), None))
    return jax.shard_map(
        per_device, mesh=mesh, in_specs=in_specs, out_specs=out_specs, check_vma=False
    )
```

```python
import math

import jax
import jax.numpy as jnp
from jax import lax
from jax.experimental import pallas as pl
from jax.experimental.pallas import tpu as pltpu
from jax.sharding import PartitionSpec as P

TILE = 128
FEAT = 256
NY, NZ, NX = 8, 3, 4
NH, NC = 4, 2
SLOTS = 24
RT = NH * NC
CT = NY * NZ * NX
NSEM = 240
MESH = pl.DeviceIdType.MESH
HIGHEST = lax.Precision.HIGHEST
F32 = jnp.float32
BF16 = jnp.bfloat16
FIRST = pl.ds(0, 32)
SECOND = pl.ds(32, 64)
UPPER = pl.ds(32, 32)
LOWER = pl.ds(64, 32)
THIRD = pl.ds(96, 32)
AHEAD = pl.ds(0, 96)
HALVES = (pl.ds(0, 64), pl.ds(64, 64))
GROUPS = ((4,), (3, -3), (2, -2), (1, -1), (0,))


def way_of(s):
    return 1 if s > 0 else -1


def split(values):
    high = values.astype(BF16)
    return high, (values - high.astype(F32)).astype(BF16)


def split_dot(values, high, low):
    top, rest = split(values)
    small = jnp.dot(top, low, preferred_element_type=F32) + jnp.dot(rest, high, preferred_element_type=F32)
    return jnp.dot(top, high, preferred_element_type=F32) + small


def kernel(places, links, feat_in, weight_in, bias_in, cot_in, vals_in, out_to, gw_to, gb_to, gin_to,
           out, gw, gb, gin, weight, bias, cot, vals,
           wsplit, gath, flip, acc, part, hpart, hcore, hline, grow,
           ring_p, line_p, line_q, ring_q, line_c, ring_c, last_c, zline,
           wbuf, wcore, wx, wy, wz, wh, wout, ssem, rsem, lsem):
    row = lax.axis_index("row")
    col = lax.axis_index("col")
    y, z, x = row // (NZ * NX), (row // NX) % NZ, row % NX
    h, c = col // NC, col % NC

    def at_x(s):
        return lax.rem(x + s + NX, NX)

    def at_y(s):
        return lax.rem(y + s + NY, NY)

    def at_z(s):
        return lax.rem(z + s, NZ)

    def at_h(s):
        return lax.rem(h + s + NH, NH)

    def to_x(s):
        return ((y * NZ + z) * NX + at_x(s), col)

    def to_y(s):
        return ((at_y(s) * NZ + z) * NX + x, col)

    def to_z(s):
        return ((y * NZ + at_z(s)) * NX + x, col)

    def to_h(index):
        return (row, index * NC + c)

    other_core = 1 - c
    partner = (row, h * NC + other_core)
    turn = 1 - 2 * c
    near = at_h(turn)
    back = at_h(-turn)
    far = at_h(2)

    copies = []

    def send(src, dst, target):
        index = len(copies)
        copy = pltpu.make_async_remote_copy(
            src_ref=src, dst_ref=dst, send_sem=ssem.at[index], recv_sem=rsem.at[index],
            device_id=target, device_id_type=MESH)
        copy.start()
        copies.append(copy)
        return copy

    def fetch(src, dst, index):
        copy = pltpu.make_async_copy(src, dst, lsem.at[index])
        copy.start()
        return copy

    barrier = pltpu.get_barrier_semaphore()
    friends = [to_x(s) for s in (1, 2, 3)] + [to_y(s) for s in range(1, NY)]
    friends += [to_z(s) for s in (1, 2)] + [to_h(at_h(s)) for s in (1, 2, 3)] + [partner]
    for friend in friends:
        pl.semaphore_signal(barrier, inc=1, device_id=friend, device_id_type=MESH)
    own_copy = fetch(feat_in, gath.at[y, z, x], 0)
    fetched = [fetch(vals_in, vals, 1), fetch(weight_in, weight, 2), fetch(cot_in, cot, 3), fetch(bias_in, bias, 4)]
    acc[SLOTS] = jnp.zeros((TILE, FEAT), F32)
    own_copy.wait()
    pl.semaphore_wait(barrier, len(friends))

    def both(up, down):
        return send(up, up, to_y(1)), send(down, down, to_y(-1))

    def ring(view, half, s, arrived):
        for cp in arrived:
            cp.wait_recv()
        if s < 3:
            return both(view(at_y(-s)), view(at_y(s)))
        if s == 3:
            return both(half(at_y(-s), 0), half(at_y(s), 1))
        return None

    def p_view(yd):
        return gath.at[yd, :, :, FIRST, :]

    def p_half(yd, i):
        return gath.at[yd, :, 2 * i:2 * i + 2, FIRST, :]

    def q_view(yd):
        return gath.at[yd, :, x, SECOND, :]

    def q_half(yd, i):
        return gath.at[yd, :, x, (UPPER, LOWER)[i], :]

    def c_view(yd):
        return gath.at[yd, z, :, THIRD, :]

    def c_half(yd, i):
        return gath.at[yd, z, 2 * i:2 * i + 2, THIRD, :]

    def q_direct(s):
        block = gath.at[at_y(s), :, x, SECOND, :]
        return {1: send(block, block, to_x(1)), -1: send(block, block, to_x(-1))}

    def q_forward(s, arrived):
        way = way_of(s)
        arrived[way].wait_recv()
        block = gath.at[at_y(s), :, at_x(-way), SECOND, :]
        return [arrived[-way], send(block, block, to_x(way))]

    def c_direct(s):
        block = gath.at[at_y(s), z, :, THIRD, :]
        return [send(block, block, to_z(1)), send(block, block, to_z(2))]

    own = gath.at[y, z, x, AHEAD, :]
    zs = [send(own, own, to_z(s)) for s in (1, 2)]
    own = gath.at[y, z, x, THIRD, :]
    xs = [send(own, own, to_x(s)) for s in (1, 2, 3)]
    pending = []
    for cp in zs:
        cp.wait_recv()
    q_ring = both(q_view(y), q_view(y))
    own = gath.at[y, :, x, FIRST, :]
    px = [send(own, own, to_x(s)) for s in (1, 2, 3)]
    for cp in xs:
        cp.wait_recv()
    c_ring = both(c_view(y), c_view(y))
    direct = {0: q_direct(0)}
    pending += c_direct(0)
    for cp in fetched:
        cp.wait()
    turned = weight[...].T
    wsplit[0], wsplit[1] = split(weight[...])
    wsplit[2], wsplit[3] = split(turned)
    p_ring = None
    for s in (1, 2, 3, 4):
        current = GROUPS[4 - s]
        q_ring = ring(q_view, q_half, s, q_ring)
        for t in current:
            direct[t] = q_direct(t)
        c_ring = ring(c_view, c_half, s, c_ring)
        for t in current:
            pending += c_direct(t)
        if s == 1:
            for cp in px:
                cp.wait_recv()
            p_ring = both(p_view(y), p_view(y))
        for t in GROUPS[5 - s]:
            pending += q_forward(t, direct[t])
        if s > 1:
            p_ring = ring(p_view, p_half, s - 1, p_ring)
    pending += q_forward(4, direct[4])
    ring(p_view, p_half, 4, p_ring)
    for cp in pending:
        cp.wait_recv()

    for k in range(SLOTS):
        spot = places[k] % CT
        block = gath[spot // (NZ * NX), (spot // NX) % NZ, spot % NX]
        value = jnp.dot(vals[k], block, preferred_element_type=F32)
        acc[k] = value + acc[links[k]]
    for r in range(RT):
        hpart[r % NC, r // NC] = acc[links[SLOTS + r]].astype(BF16)

    cp = send(hpart.at[other_core], hcore, partner)
    for k in range(0, 8):
        flip[k] = vals[k].T
    cp.wait_recv()
    hpart[c] = hpart[c] + hcore[...]
    legs = [send(hpart.at[c, far, half, :], hline.at[0, half, :], to_h(near)) for half in HALVES]
    for k in range(8, 16):
        flip[k] = vals[k].T
    plain = send(hpart.at[c, back], hline.at[1], to_h(back))
    summed = []
    for leg, half in zip(legs, HALVES):
        leg.wait_recv()
        hpart[c, near, half, :] = hpart[c, near, half, :] + hline[0, half, :]
        summed.append(send(hpart.at[c, near, half, :], hline.at[2, half, :], to_h(near)))
    hidden = acc[links[SLOTS + col]] + hcore[h].astype(F32)
    for k in range(16, 24):
        flip[k] = vals[k].T
    plain.wait_recv()
    hidden = hidden + hline[1].astype(F32)
    for cp in summed:
        cp.wait_recv()
    hidden = hidden + hline[2].astype(F32)

    pre_act = split_dot(hidden, wsplit[0], wsplit[1]) + bias[...]
    sig = jax.nn.sigmoid(pre_act)
    slope = sig * (1.0 + pre_act * (1.0 - sig))
    grad_pre = (cot[...].astype(F32) * slope).astype(BF16)
    grow[h, c] = grad_pre

    own = grow.at[h, c]
    aheads = []
    for half in HALVES:
        block = grow.at[h, c, half, :]
        aheads.append(send(block, block, to_h(near)))
    over = [send(own, own, partner)]
    out[...] = (pre_act * sig).astype(BF16)
    stored = [fetch(out, out_to, 5)]
    behind = send(own, own, to_h(back))
    factor = 1.0 / math.sqrt(TILE * NY * NZ * NX * NH * NC)
    grad_float = grad_pre.astype(F32)
    local = lax.dot_general(hidden, grad_float, (((0,), (0,)), ((), ())), precision=HIGHEST,
                            preferred_element_type=F32)
    local_bias = jnp.sum(grad_float, axis=0, keepdims=True)
    for cc in range(NC):
        cols = slice(cc * TILE, (cc + 1) * TILE)
        wbuf[cc, :, :, 0:8, :] = local[:, cols].reshape(NX, NY, 8, TILE)
        wbuf[cc, :, :, 8:16, :] = jnp.broadcast_to(local_bias[:, cols].reshape(1, 1, 1, TILE), (NX, NY, 8, TILE))
    w_core = send(wbuf.at[other_core], wcore, partner)
    onward = []
    for ahead, half in zip(aheads, HALVES):
        ahead.wait_recv()
        block = grow.at[back, c, half, :]
        onward.append(send(block, block, to_h(near)))
    block = grow.at[back, c]
    over.append(send(block, block, partner))
    behind.wait_recv()
    block = grow.at[near, c]
    over.append(send(block, block, partner))
    w_core.wait_recv()
    wbuf[c] = wbuf[c] + wcore[...]
    w_x = [send(wbuf.at[c, at_x(s)], wx.at[s - 1], to_x(s)) for s in (1, 2, 3)]
    for cp in onward:
        cp.wait_recv()
    block = grow.at[far, c]
    over.append(send(block, block, partner))
    for cp in w_x:
        cp.wait_recv()
    wbuf[c, x] = wbuf[c, x] + wx[0] + wx[1] + wx[2]
    w_y = [send(wbuf.at[c, x, at_y(s)], wy.at[s - 1], to_y(s)) for s in range(1, NY)]
    for cp in over:
        cp.wait_recv()

    for k in range(SLOTS):
        spot = places[k] // CT
        value = jnp.dot(flip[k], grow[spot // NC, spot % NC], preferred_element_type=F32)
        acc[k] = value + acc[links[SLOTS + RT + k]]

    def fill(s):
        yd = at_y(s)
        for zi in range(NZ):
            for xi in range(NX):
                place = (yd * NZ + zi) * NX + xi
                part[yd, zi, xi] = acc[links[2 * SLOTS + RT + place]].astype(BF16)

    def add(dst, src):
        dst[...] = dst[...] + src[...]

    def add3(dst, one, two):
        dst[...] = (dst[...].astype(F32) + one[...].astype(F32) + two[...].astype(F32)).astype(BF16)

    def q_start(s):
        way, place = way_of(s), len(started)
        leg = send(part.at[at_y(s), :, at_x(2), SECOND, :], line_q.at[place, 0], to_x(way))
        straight = send(part.at[at_y(s), :, at_x(-way), SECOND, :], line_q.at[place, 1], to_x(-way))
        lines = [send(part.at[at_y(s), at_z(d), :, THIRD, :], line_c.at[place, d - 1], to_z(d)) for d in (1, 2)]
        started[s] = place, leg, straight, lines

    def q_middle(s):
        way = way_of(s)
        place, leg, _, _ = started[s]
        leg.wait_recv()
        block = part.at[at_y(s), :, at_x(way), SECOND, :]
        add(block, line_q.at[place, 0])
        middle[s] = send(block, line_q.at[place, 2], to_x(way))

    def q_end(s):
        place, _, straight, _ = started[s]
        straight.wait_recv()
        middle[s].wait_recv()
        add3(part.at[at_y(s), :, x, SECOND, :], line_q.at[place, 1], line_q.at[place, 2])

    def c_end(s):
        place, _, _, lines = started[s]
        for cp in lines:
            cp.wait_recv()
        add3(part.at[at_y(s), z, :, THIRD, :], line_c.at[place, 0], line_c.at[place, 1])

    def ring_sum(view, half, slot, slot_half, t, arrived):
        if t >= 1:
            for cp in arrived:
                cp.wait_recv()
            if t == 1:
                add(half(at_y(3), 0), slot_half(0))
                add(half(at_y(-3), 1), slot_half(1))
            elif t < 4:
                add(view(at_y(4 - t)), slot(0, t - 1))
                add(view(at_y(t - 4)), slot(1, t - 1))
            else:
                add3(view(y), slot(0, 3), slot(1, 3))
        if t == 0:
            return send(half(at_y(4), 0), slot_half(0), to_y(1)), send(half(at_y(4), 1), slot_half(1), to_y(-1))
        if t < 4:
            return (send(view(at_y(4 - t)), slot(0, t), to_y(1)), send(view(at_y(t - 4)), slot(1, t), to_y(-1)))
        return None

    p_args = (lambda yd: part.at[yd, :, :, FIRST, :],
              lambda yd, i: part.at[yd, :, 2 * i:2 * i + 2, FIRST, :],
              lambda i, t: ring_p.at[i, t],
              lambda i: ring_p.at[i, 0, :, 2 * i:2 * i + 2])
    q_args = (lambda yd: part.at[yd, :, x, SECOND, :],
              lambda yd, i: part.at[yd, :, x, (UPPER, LOWER)[i], :],
              lambda i, t: ring_q.at[i, t],
              lambda i: ring_q.at[i, 0, :, pl.ds(32 * i, 32)])
    c_args = (lambda yd: part.at[yd, z, :, THIRD, :],
              lambda yd, i: part.at[yd, z, 2 * i:2 * i + 2, THIRD, :],
              lambda i, t: ring_c.at[i, t],
              lambda i: ring_c.at[i, 0, 2 * i:2 * i + 2])
    started, middle = {}, {}
    fill(4)
    p_ring = ring_sum(*p_args, 0, None)
    q_start(4)
    for group in GROUPS[1:]:
        for s in group:
            fill(s)
        if group[0] == 3:
            for s in group:
                q_start(s)
    q_middle(4)

    for cp in w_y:
        cp.wait_recv()
    wz[z] = wbuf[c, x, y] + jnp.sum(wy[...], axis=0)
    w_z = [send(wz.at[z], wz.at[z], to_z(s)) for s in (1, 2)]

    q_ring = c_ring = None
    for t in (0, 1, 2, 3, 4):
        if t < 3:
            for s in GROUPS[t + 2]:
                q_start(s)
        if t >= 1:
            p_ring = ring_sum(*p_args, t, p_ring)
        if t == 4:
            px = [send(part.at[y, :, at_x(s), FIRST, :], line_p.at[s - 1], to_x(s)) for s in (1, 2, 3)]
        for s in GROUPS[t]:
            c_end(s)
        c_ring = ring_sum(*c_args, t, c_ring)
        for s in GROUPS[t]:
            q_end(s)
        q_ring = ring_sum(*q_args, t, q_ring)
        if t < 4:
            for s in GROUPS[t + 1]:
                q_middle(s)
        if t == 0:
            for cp in w_z:
                cp.wait_recv()
            wh[h] = wz[0] + wz[1] + wz[2]
            w_h = [send(wh.at[h], wh.at[h], to_h(at_h(s))) for s in (1, 2, 3)]
        elif t == 1:
            for cp in w_h:
                cp.wait_recv()
            wout[c, x, y] = (wh[0] + wh[1] + wh[2] + wh[3]) * factor
            piece = wout.at[c, x, y]
            w_y = [send(piece, piece, to_y(s)) for s in range(1, NY)]
        elif t == 2:
            for cp in w_y:
                cp.wait_recv()
            piece = wout.at[c, x]
            w_x = [send(piece, piece, to_x(s)) for s in (1, 2, 3)]
        elif t == 3:
            for cp in w_x:
                cp.wait_recv()
            w_core = send(wout.at[c], wout.at[c], partner)
    last_q = [send(part.at[y, at_z(s), x, SECOND, :], zline.at[s - 1, SECOND, :], to_z(s)) for s in (1, 2)]
    last_x = [send(part.at[y, z, at_x(s), THIRD, :], last_c.at[s - 1], to_x(s)) for s in (1, 2, 3)]
    for cp in px:
        cp.wait_recv()
    block = part.at[y, :, x, FIRST, :]
    block[...] = (block[...].astype(F32) + line_p[0].astype(F32) + line_p[1].astype(F32)
                  + line_p[2].astype(F32)).astype(BF16)
    last_p = [send(part.at[y, at_z(s), x, FIRST, :], zline.at[s - 1, FIRST, :], to_z(s)) for s in (1, 2)]
    w_core.wait_recv()
    for cc in range(NC):
        cols = slice(cc * TILE, (cc + 1) * TILE)
        gw[:, cols] = wout[cc, :, :, 0:8, :].reshape(FEAT, TILE)
        gb[:, cols] = wout[cc, 0, 0, 8:9, :]
    stored += [fetch(gw, gw_to, 7), fetch(gb, gb_to, 8)]
    for cp in last_q + last_x + last_p:
        cp.wait_recv()
    ahead_rows = part[y, z, x, AHEAD, :].astype(F32) + zline[0].astype(F32) + zline[1].astype(F32)
    third_rows = part[y, z, x, THIRD, :].astype(F32) + last_c[0].astype(F32) + last_c[1].astype(F32)
    third_rows = third_rows + last_c[2].astype(F32)
    adjoint = jnp.concatenate([ahead_rows, third_rows], axis=0)
    gin[...] = split_dot(adjoint, wsplit[2], wsplit[3]).astype(BF16)
    stored.append(fetch(gin, gin_to, 6))
    for cp in copies:
        cp.wait_send()
    for cp in stored:
        cp.wait()


def hand_over(*refs):
    given, wanted, kept, sems = refs[0:4], refs[4:8], refs[8:12], refs[12]
    moves = [pltpu.make_async_copy(given[i], kept[i], sems.at[i]) for i in range(4)]
    for move in moves:
        move.start()
    for i in range(4):
        moves[i].wait()
        moves.append(pltpu.make_async_copy(kept[i], wanted[i], sems.at[4 + i]))
        moves[4 + i].start()
    for move in moves[4:]:
        move.wait()


def per_device(features, weight, bias, cotangent, tile_values, tile_pos, tile_count):
    places = tile_pos[0, 0]
    in_use = tile_count[0, 0]
    slot = jnp.arange(SLOTS, dtype=jnp.int32)
    rows, cols = places // CT, places % CT
    full = jnp.full((CT,), SLOTS, jnp.int32)
    asked = jnp.concatenate([rows, jnp.arange(RT, dtype=jnp.int32), cols + RT, jnp.arange(CT, dtype=jnp.int32) + RT])
    limit = jnp.concatenate([slot, full[:RT], slot, full])
    limit = jnp.minimum(limit, in_use)
    same = jnp.where(asked[:, None] < RT, rows[None, :] == asked[:, None], cols[None, :] + RT == asked[:, None])
    found = jnp.max(jnp.where(same & (slot[None, :] < limit[:, None]), slot[None, :], -1), axis=1)
    links = jnp.where(found < 0, SLOTS, found)
    smem = pl.BlockSpec(memory_space=pltpu.SMEM)
    blocks = pltpu.VMEM
    scratch = [
        blocks((TILE, FEAT), BF16),
        blocks((FEAT, FEAT), F32),
        blocks((1, FEAT), F32),
        blocks((TILE, FEAT), BF16),
        blocks((FEAT, FEAT), F32),
        blocks((1, FEAT), F32),
        blocks((TILE, FEAT), BF16),
        blocks((SLOTS, TILE, TILE), BF16),
        blocks((4, FEAT, FEAT), BF16),
        blocks((NY, NZ, NX, TILE, FEAT), BF16),
        blocks((SLOTS, TILE, TILE), BF16),
        blocks((SLOTS + 1, TILE, FEAT), F32),
        blocks((NY, NZ, NX, TILE, FEAT), BF16),
        blocks((NC, NH, TILE, FEAT), BF16),
        blocks((NH, TILE, FEAT), BF16),
        blocks((3, TILE, FEAT), BF16),
        blocks((NH, NC, TILE, FEAT), BF16),
        blocks((2, 4, NZ, NX, 32, FEAT), BF16),
        blocks((3, NZ, 32, FEAT), BF16),
        blocks((NY, 3, NZ, 64, FEAT), BF16),
        blocks((2, 4, NZ, 64, FEAT), BF16),
        blocks((NY, 2, NX, 32, FEAT), BF16),
        blocks((2, 4, NX, 32, FEAT), BF16),
        blocks((3, 32, FEAT), BF16),
        blocks((2, 96, FEAT), BF16),
        blocks((NC, NX, NY, 16, TILE), F32),
        blocks((NX, NY, 16, TILE), F32),
        blocks((3, NY, 16, TILE), F32),
        blocks((NY - 1, 16, TILE), F32),
        blocks((NZ, 16, TILE), F32),
        blocks((NH, 16, TILE), F32),
        blocks((NC, NX, NY, 16, TILE), F32),
        pltpu.SemaphoreType.DMA((NSEM,)),
        pltpu.SemaphoreType.DMA((NSEM,)),
        pltpu.SemaphoreType.DMA((9,)),
    ]
    results = (
        jax.ShapeDtypeStruct((TILE, FEAT), BF16),
        jax.ShapeDtypeStruct((FEAT, FEAT), F32),
        jax.ShapeDtypeStruct((1, FEAT), F32),
        jax.ShapeDtypeStruct((TILE, FEAT), BF16),
    )
    anywhere = pl.BlockSpec(memory_space=pl.ANY)
    made = pl.pallas_call(
        kernel,
        out_shape=results,
        in_specs=[smem, smem] + [anywhere] * 5,
        out_specs=(anywhere,) * 4,
        scratch_shapes=scratch,
        compiler_params=pltpu.CompilerParams(
            collective_id=0, has_side_effects=True, vmem_limit_bytes=63 * 1024 * 1024),
    )(places, links, features, weight, bias.reshape(1, FEAT), cotangent, tile_values[0, 0])
    output, grad_weight, grad_bias, grad_input = pl.pallas_call(
        hand_over,
        out_shape=results,
        in_specs=[anywhere] * 4,
        out_specs=(anywhere,) * 4,
        scratch_shapes=scratch[:4] + [pltpu.SemaphoreType.DMA((8,))],
    )(*made)
    return output, grad_weight, grad_bias[0], grad_input


def solution(mesh):
    in_specs = (
        P(("row", "col"), None),
        P(),
        P(),
        P(("row", "col"), None),
        P("row", "col", None, None, None),
        P("row", "col", None),
        P("row", "col"),
    )
    out_specs = (P(("row", "col"), None), P(), P(), P(("row", "col"), None))
    return jax.shard_map(
        per_device, mesh=mesh, in_specs=in_specs, out_specs=out_specs, check_vma=False
    )
```
